32 devices in a mesh: chan: 8 (over y, x, core), freq: 4 (over z).
Axes of the slice: x: 2, y: 2, z: 4, core: 2. Of those that a mesh axis runs over, the one named last changes fastest.
Arguments:
- raw: bfloat16 [1280, 8192], P('chan', 'freq')
- good_list: int32 [1024], P('chan'), may hold values from 0 to 159, as said below
- dest: int32 [1024], P('chan'), may hold values from 0 to 7, as said below
- order: int32 [4], replicated, may hold values from 0 to 7, as said below
- picks: int32 [4, 2], replicated, may hold values from 0 to 255, as said below
Outputs:
- corr: float32 [2048, 8, 512], P('chan', None, 'freq')
The draws below stay inside these ranges and needn't reach their ends.
Inputs may be any that keep to these rules, and one draw needn't show every extreme that they name: `good_list`: the 128 entries of one device are distinct local rows of its 160 recorded rows. `dest`: the entries of one device name each block either exactly 32 times or not at all; each block is named by exactly half of the devices. `order`: the 4 entries are distinct blocks. Each pick names a slot of block order[t] that a listed channel fills; the picks of one step are distinct.
All inputs are finite; a program needn't handle non-finite values.
Results may differ from the reference program's by a relative error of at most 0.0061.
Values may be sent and summed in bfloat16 or wider, within the bound.
A program may use at most 64 MiB of HBM per device.

```python
import math
import jax
import jax.numpy as jnp
from jax import lax

W = 1024
LAGS = 512
GOOD_DEV = 128
RAW_DEV = 160
SWD = 2
STEPS = 4
SP = 2
N_CHAN = 8
N_FREQ = 4


def block_layout(key):
    key_relabel, key_offsets, key_order, key_place = jax.random.split(key, 4)
    relabel = jax.random.permutation(key_relabel, N_CHAN).astype(jnp.int32)
    inverse = jnp.argsort(relabel, stable=True).astype(jnp.int32)
    needed = ((inverse[N_CHAN - 1] + 1) % N_CHAN).astype(jnp.int32)
    others = (needed + 1 + jax.random.permutation(key_offsets, N_CHAN - 1)[:N_CHAN // 2 - 1].astype(jnp.int32)) % N_CHAN
    offsets = jnp.concatenate([needed[None], others.astype(jnp.int32)]).astype(jnp.int32)
    rest = jax.random.permutation(key_order, N_CHAN - 1)[:STEPS - 1].astype(jnp.int32)
    listed = jnp.concatenate([jnp.full((1,), N_CHAN - 1, jnp.int32), rest])
    chosen = listed[jax.random.permutation(key_place, STEPS)].astype(jnp.int32)
    return (relabel, offsets, chosen)


def draw_raw(key, part):
    key = jax.random.fold_in(key, 19)
    key_amp, key_noise = jax.random.split(key, 2)
    row_total = N_CHAN * RAW_DEV
    col_total = SWD * N_FREQ * W
    amplitude = jnp.exp(jax.random.uniform(key_amp, (row_total, 1), jnp.float32, math.log(0.1), math.log(10.0)))
    values = jnp.clip(jax.random.normal(key_noise, (row_total, col_total), jnp.float32), -5.0, 5.0) * amplitude
    return values.astype(jnp.bfloat16)


def draw_good_list(key, part):
    key = jax.random.fold_in(key, 17)
    device_keys = jax.random.split(key, N_CHAN)
    lists = jax.vmap(lambda one_key: jax.random.permutation(one_key, RAW_DEV)[:GOOD_DEV])(device_keys)
    return lists.reshape(-1).astype(jnp.int32)


def draw_dest(key, part):
    relabel, offsets, chosen = block_layout(key)
    key = jax.random.fold_in(key, 11)
    capacity = 2 * GOOD_DEV // N_CHAN
    devices = jnp.arange(N_CHAN, dtype=jnp.int32)[:, None]
    targets = relabel[(devices + offsets[None, :]) % N_CHAN]
    repeated = jnp.repeat(targets, capacity, axis=1)
    device_keys = jax.random.split(key, N_CHAN)
    shuffled = jax.vmap(lambda one_key, row_vals: jax.random.permutation(one_key, row_vals))(device_keys, repeated)
    return shuffled.reshape(-1).astype(jnp.int32)


def draw_order(key, part):
    relabel, offsets, chosen = block_layout(key)
    return chosen


def draw_picks(key, part):
    relabel, offsets, chosen = block_layout(key)
    key = jax.random.fold_in(key, 23)
    capacity = 2 * GOOD_DEV // N_CHAN
    half_count = N_CHAN // 2
    inverse = jnp.argsort(relabel, stable=True).astype(jnp.int32)
    key_sel, key_slot = jax.random.split(key)
    step_keys = jax.random.split(key_sel, STEPS)
    selected = jax.vmap(lambda one_key: jax.random.permutation(one_key, half_count)[:SP])(step_keys).astype(jnp.int32)
    rotated = (selected + (half_count - selected[:, :1])) % half_count
    is_last = (chosen == N_CHAN - 1)[:, None]
    selected = jnp.where(is_last, rotated, selected)
    shifts = offsets[selected]
    senders = (inverse[chosen][:, None] - shifts) % N_CHAN
    within = jax.random.randint(key_slot, (STEPS, SP), 0, capacity).astype(jnp.int32)
    first_col = (jnp.arange(SP, dtype=jnp.int32) == 0)[None, :]
    within = jnp.where(jnp.logical_and(is_last, first_col), capacity - 1, within)
    return (senders * capacity + within).astype(jnp.int32)


def setup_inputs(seed: int = 0) -> dict:
    arg_keys = jax.random.split(jax.random.key(seed), 6)
    return {
        "raw": draw_raw(jax.random.fold_in(arg_keys[5], 71), 0),
        "good_list": draw_good_list(jax.random.fold_in(arg_keys[5], 71), 0),
        "dest": draw_dest(jax.random.fold_in(arg_keys[5], 71), 0),
        "order": draw_order(jax.random.fold_in(arg_keys[5], 71), 0),
        "picks": draw_picks(jax.random.fold_in(arg_keys[5], 71), 0),
    }


power_floor = 0.1

def transform_table(bands):
    sample = jnp.arange(W, dtype=jnp.int32)[:, None]
    column = jnp.arange(W, dtype=jnp.int32)[None, :]
    width_band = W // bands
    half_band = width_band // 2
    band_index = column // width_band
    within = column % width_band
    half_index = within // half_band
    bin_index = band_index * half_band + within % half_band
    residue = jnp.mod(sample * bin_index, W).astype(jnp.float32)
    phase_rad = residue * (2.0 * math.pi / W)
    taper = 0.5 - 0.5 * jnp.cos(sample.astype(jnp.float32) * (2.0 * math.pi / W))
    entries = jnp.where(half_index == 0, jnp.cos(phase_rad), -jnp.sin(phase_rad)) * taper * (1.0 / math.sqrt(W))
    return entries.astype(jnp.bfloat16)

def lag_rows(row_index, lag_index, half_band, scale):
    band_index = row_index // (2 * half_band)
    within = row_index % (2 * half_band)
    half_index = within // half_band
    bin_index = band_index * half_band + within % half_band
    lag_shift = lag_index - LAGS // 2
    residue = jnp.mod(bin_index[:, None] * lag_shift[None, :], W).astype(jnp.float32)
    phase_rad = residue * (2.0 * math.pi / W)
    entries = jnp.where(half_index[:, None] == 0, jnp.cos(phase_rad), -jnp.sin(phase_rad)) * scale
    return entries.astype(jnp.bfloat16)

def whiten(spectra):
    values = spectra.astype(jnp.float32)
    half_band = values.shape[-1] // 2
    real_part = values[..., :half_band]
    imag_part = values[..., half_band:]
    band_power = lax.optimization_barrier(jnp.mean(real_part * real_part + imag_part * imag_part, axis=1, keepdims=True))
    factor = 1.0 / jnp.sqrt(jnp.maximum(band_power, power_floor))
    return (values * jnp.concatenate([factor, factor], axis=-1)).astype(jnp.bfloat16)

def cross(whitened, panel):
    half_band = whitened.shape[-1] // 2
    left = whitened.astype(jnp.float32)
    right = panel.astype(jnp.float32)
    left_re, left_im = (left[..., :half_band], left[..., half_band:])
    right_re, right_im = (right[..., :half_band], right[..., half_band:])
    high = lax.Precision.HIGHEST
    real_part = jnp.einsum('isbf,jsbf->ijbf', left_re, right_re, precision=high) + jnp.einsum('isbf,jsbf->ijbf', left_im, right_im, precision=high)
    imag_part = jnp.einsum('isbf,jsbf->ijbf', left_im, right_re, precision=high) - jnp.einsum('isbf,jsbf->ijbf', left_re, right_im, precision=high)
    return jnp.concatenate([real_part, imag_part], axis=-1).astype(jnp.bfloat16)

def reference(raw, good_list, dest, order, picks):
    n_chan = N_CHAN
    n_freq = N_FREQ
    capacity = 2 * GOOD_DEV // n_chan
    slot_count = n_chan * capacity
    total_sub = SWD * n_freq
    width_band = W // n_freq
    device_dest = dest.reshape(n_chan, GOOD_DEV)
    device_good = good_list.reshape(n_chan, GOOD_DEV)
    positions = jnp.arange(GOOD_DEV, dtype=jnp.int32)
    matching = device_dest[:, :, None] == device_dest[:, None, :]
    before = positions[None, :] < positions[:, None]
    earlier_count = lax.optimization_barrier(jnp.sum(jnp.logical_and(matching, before[None, :, :]), axis=2)).astype(jnp.int32)
    devices = jnp.arange(n_chan, dtype=jnp.int32)[:, None]
    slot_index = device_dest * slot_count + devices * capacity + earlier_count
    source_row = devices * RAW_DEV + device_good
    row_table = jnp.full((n_chan * slot_count,), -1, dtype=jnp.int32)
    row_table = row_table.at[slot_index.reshape(-1)].set(source_row.reshape(-1).astype(jnp.int32))
    raw_sub = raw.reshape(n_chan * RAW_DEV, total_sub, W)
    trans = transform_table(n_freq)

    def white_block(block_id):
        first_slot = (block_id * slot_count).astype(jnp.int32)
        row_ids = lax.dynamic_slice(row_table, (first_slot,), (slot_count,))
        rows = raw_sub[jnp.maximum(row_ids, 0)]
        rows = jnp.where(row_ids[:, None, None] >= 0, rows, jnp.zeros_like(rows))
        spectra = jnp.dot(rows.reshape(slot_count * total_sub, W), trans, preferred_element_type=jnp.float32)
        spectra = spectra.astype(jnp.bfloat16).reshape(slot_count, total_sub, n_freq, width_band)
        return whiten(spectra)
    source_blocks = lax.map(white_block, order.astype(jnp.int32))
    panels = source_blocks[jnp.arange(STEPS)[:, None], picks]
    panels = panels.reshape(STEPS * SP, total_sub, n_freq, width_band)
    scale = 1.0 / math.sqrt(total_sub * (W // 2))
    lag_table = lag_rows(jnp.arange(W, dtype=jnp.int32), jnp.arange(LAGS, dtype=jnp.int32), width_band // 2, scale)

    def corr_block(block_id):
        spectra_cross = cross(white_block(block_id), panels).reshape(slot_count * STEPS * SP, W)
        result = jnp.dot(spectra_cross, lag_table, preferred_element_type=jnp.float32)
        return result.reshape(slot_count, STEPS * SP, LAGS)
    blocks_out = lax.map(corr_block, jnp.arange(n_chan, dtype=jnp.int32))
    return blocks_out.reshape(n_chan * slot_count, STEPS * SP, LAGS)
```

```python
import math

import jax
import jax.numpy as jnp
import ml_dtypes
import numpy as np
from jax import lax
from jax.sharding import PartitionSpec as P

W = 1024
LAGS = 512


power_floor = 0.1


def transform_table(bands):
    sample = np.arange(W, dtype=np.int64)[:, None]
    column = np.arange(W, dtype=np.int64)[None, :]
    width_band = W // bands
    half_band = width_band // 2
    within = column % width_band
    bin_index = (column // width_band) * half_band + within % half_band
    phase_rad = ((sample * bin_index) % W) * (2.0 * math.pi / W)
    taper = 0.5 - 0.5 * np.cos(sample * (2.0 * math.pi / W))
    entries = np.where(within < half_band, np.cos(phase_rad), -np.sin(phase_rad))
    return (entries * taper / math.sqrt(W)).astype(np.float32).astype(ml_dtypes.bfloat16)


def lag_rows(bands, scale):
    row_index = np.arange(W, dtype=np.int64)
    width_band = W // bands
    half_band = width_band // 2
    within = row_index % width_band
    bin_index = (row_index // width_band) * half_band + within % half_band
    lag_shift = np.arange(LAGS, dtype=np.int64) - LAGS // 2
    phase_rad = ((bin_index[:, None] * lag_shift[None, :]) % W) * (2.0 * math.pi / W)
    entries = np.where(within[:, None] < half_band, np.cos(phase_rad), -np.sin(phase_rad))
    return (entries * scale).astype(np.float32).astype(ml_dtypes.bfloat16)


def whiten(spectra):
    values = spectra.astype(jnp.float32)
    band_power = jnp.mean(jnp.sum(values * values, axis=-2, keepdims=True), axis=-3, keepdims=True)
    factor = 1.0 / jnp.sqrt(jnp.maximum(band_power, power_floor))
    return (values * factor).astype(jnp.bfloat16)


def body(raw, good_list, dest, order, picks):
    n_chan = lax.axis_size("chan")
    n_freq = lax.axis_size("freq")
    good_count = good_list.shape[0]
    raw_rows = raw.shape[0]
    capacity = 2 * good_count // n_chan
    slot_count = n_chan * capacity
    sub_count = raw.shape[1] // W
    total_sub = sub_count * n_freq
    steps, per_step = picks.shape
    sources = steps * per_step
    share = good_count // n_freq
    positions = jnp.arange(good_count, dtype=jnp.int32)
    matching = dest[:, None] == dest[None, :]
    earlier_count = jnp.sum(
        jnp.logical_and(matching, positions[None, :] < positions[:, None]), axis=1
    )
    slot_index = dest * capacity + earlier_count
    row_onehot = (good_list[:, None] == jnp.arange(raw_rows, dtype=jnp.int32)[None, :]).astype(
        jnp.bfloat16
    )
    slot_onehot = (jnp.arange(slot_count, dtype=jnp.int32)[:, None] == slot_index[None, :]).astype(
        jnp.bfloat16
    )
    block = jnp.repeat(order, per_step)
    pick = picks.reshape(sources)
    mine = pick // capacity == lax.axis_index("chan")
    source_slot = jnp.where(mine, block * capacity + pick % capacity, -1)
    source_onehot = (source_slot[:, None] == slot_index[None, :]).astype(jnp.bfloat16)

    good = jnp.dot(row_onehot, raw, preferred_element_type=jnp.float32).astype(jnp.bfloat16)
    panel_raw = jnp.dot(source_onehot, good, preferred_element_type=jnp.float32).astype(jnp.bfloat16)
    panel_raw = lax.psum(panel_raw, "chan")
    panel_raw = lax.all_gather(panel_raw.reshape(sources, sub_count, W), "freq", axis=1, tiled=True)

    rows = lax.all_to_all(
        good.reshape(n_freq, share, sub_count, W), "freq", split_axis=0, concat_axis=2, tiled=True
    )
    rows = rows.reshape(share, total_sub, W)
    trans = jnp.asarray(transform_table(n_freq))
    half_band = W // n_freq // 2

    def white(values):
        spectra = jnp.einsum("cmw,wk->cmk", values, trans, preferred_element_type=jnp.float32)
        spectra = spectra.astype(jnp.bfloat16).reshape(-1, total_sub, n_freq, 2, half_band)
        spectra = spectra.transpose(0, 1, 3, 2, 4).reshape(-1, total_sub, 2, W // 2)
        return whiten(spectra).astype(jnp.float32)

    panels = white(panel_raw)
    whitened = white(rows)
    left_re, left_im = whitened[:, None, :, 0], whitened[:, None, :, 1]
    right_re, right_im = panels[None, :, :, 0], panels[None, :, :, 1]
    real_part = jnp.sum(left_re * right_re + left_im * right_im, axis=2)
    imag_part = jnp.sum(left_im * right_re - left_re * right_im, axis=2)
    spectra_cross = jnp.concatenate([real_part, imag_part], axis=-1).astype(jnp.bfloat16)
    scale = 1.0 / math.sqrt(total_sub * (W // 2))
    table = lag_rows(n_freq, scale).reshape(n_freq, 2, half_band, LAGS)
    table = jnp.asarray(table.transpose(1, 0, 2, 3).reshape(W, LAGS))
    corr = jnp.einsum("ijf,fl->ijl", spectra_cross, table, preferred_element_type=jnp.float32)
    corr = lax.all_to_all(
        corr.astype(jnp.bfloat16), "freq", split_axis=2, concat_axis=0, tiled=True
    )
    lags = LAGS // n_freq
    placed = jnp.dot(
        slot_onehot, corr.reshape(good_count, sources * lags), preferred_element_type=jnp.float32
    ).astype(jnp.bfloat16)
    placed = placed.reshape(n_chan, capacity, sources, lags)
    received = lax.all_to_all(placed, "chan", split_axis=0, concat_axis=0, tiled=True)
    return received.reshape(slot_count, sources, lags).astype(jnp.float32)


def solution(mesh):
    placed = (P("chan", "freq"), P("chan"), P("chan"), P(), P())
    return jax.shard_map(
        body, mesh=mesh, in_specs=placed, out_specs=P("chan", None, "freq"), check_vma=False
    )
```

```python
import functools
import math

import jax
import jax.numpy as jnp
import ml_dtypes
import numpy as np
from jax import lax
from jax.experimental import pallas as pl
from jax.experimental.pallas import tpu as pltpu
from jax.sharding import PartitionSpec as P

W = 1024
LAGS = 512


power_floor = 0.1


def transform_table(bands):
    sample = np.arange(W, dtype=np.int64)[:, None]
    column = np.arange(W, dtype=np.int64)[None, :]
    width_band = W // bands
    half_band = width_band // 2
    within = column % width_band
    bin_index = (column // width_band) * half_band + within % half_band
    phase_rad = ((sample * bin_index) % W) * (2.0 * math.pi / W)
    taper = 0.5 - 0.5 * np.cos(sample * (2.0 * math.pi / W))
    entries = np.where(within < half_band, np.cos(phase_rad), -np.sin(phase_rad))
    return (entries * taper / math.sqrt(W)).astype(np.float32).astype(ml_dtypes.bfloat16)


def lag_rows(bands, scale):
    row_index = np.arange(W, dtype=np.int64)
    width_band = W // bands
    half_band = width_band // 2
    within = row_index % width_band
    bin_index = (row_index // width_band) * half_band + within % half_band
    lag_shift = np.arange(LAGS, dtype=np.int64) - LAGS // 2
    phase_rad = ((bin_index[:, None] * lag_shift[None, :]) % W) * (2.0 * math.pi / W)
    entries = np.where(within[:, None] < half_band, np.cos(phase_rad), -np.sin(phase_rad))
    return (entries * scale).astype(np.float32).astype(ml_dtypes.bfloat16)


def whiten(spectra):
    values = spectra.astype(jnp.float32)
    band_power = jnp.mean(jnp.sum(values * values, axis=-2, keepdims=True), axis=-3, keepdims=True)
    factor = 1.0 / jnp.sqrt(jnp.maximum(band_power, power_floor))
    return (values * factor).astype(jnp.bfloat16)


def separate(raw, good_list, dest, order, picks):
    n_chan = lax.axis_size("chan")
    n_freq = lax.axis_size("freq")
    good_count = good_list.shape[0]
    raw_rows = raw.shape[0]
    capacity = 2 * good_count // n_chan
    slot_count = n_chan * capacity
    sub_count = raw.shape[1] // W
    total_sub = sub_count * n_freq
    steps, per_step = picks.shape
    sources = steps * per_step
    share = good_count // n_freq
    positions = jnp.arange(good_count, dtype=jnp.int32)
    matching = dest[:, None] == dest[None, :]
    earlier_count = jnp.sum(
        jnp.logical_and(matching, positions[None, :] < positions[:, None]), axis=1
    )
    slot_index = dest * capacity + earlier_count
    row_onehot = (good_list[:, None] == jnp.arange(raw_rows, dtype=jnp.int32)[None, :]).astype(
        jnp.bfloat16
    )
    slot_onehot = (jnp.arange(slot_count, dtype=jnp.int32)[:, None] == slot_index[None, :]).astype(
        jnp.bfloat16
    )
    block = jnp.repeat(order, per_step)
    pick = picks.reshape(sources)
    mine = pick // capacity == lax.axis_index("chan")
    source_slot = jnp.where(mine, block * capacity + pick % capacity, -1)
    source_onehot = (source_slot[:, None] == slot_index[None, :]).astype(jnp.bfloat16)

    good = jnp.dot(row_onehot, raw, preferred_element_type=jnp.float32).astype(jnp.bfloat16)
    panel_raw = jnp.dot(source_onehot, good, preferred_element_type=jnp.float32).astype(jnp.bfloat16)
    panel_raw = lax.psum(panel_raw, "chan")
    panel_raw = lax.all_gather(panel_raw.reshape(sources, sub_count, W), "freq", axis=1, tiled=True)

    rows = lax.all_to_all(
        good.reshape(n_freq, share, sub_count, W), "freq", split_axis=0, concat_axis=2, tiled=True
    )
    rows = rows.reshape(share, total_sub, W)
    trans = jnp.asarray(transform_table(n_freq))
    half_band = W // n_freq // 2

    def white(values):
        spectra = jnp.einsum("cmw,wk->cmk", values, trans, preferred_element_type=jnp.float32)
        spectra = spectra.astype(jnp.bfloat16).reshape(-1, total_sub, n_freq, 2, half_band)
        spectra = spectra.transpose(0, 1, 3, 2, 4).reshape(-1, total_sub, 2, W // 2)
        return whiten(spectra).astype(jnp.float32)

    panels = white(panel_raw)
    whitened = white(rows)
    left_re, left_im = whitened[:, None, :, 0], whitened[:, None, :, 1]
    right_re, right_im = panels[None, :, :, 0], panels[None, :, :, 1]
    real_part = jnp.sum(left_re * right_re + left_im * right_im, axis=2)
    imag_part = jnp.sum(left_im * right_re - left_re * right_im, axis=2)
    spectra_cross = jnp.concatenate([real_part, imag_part], axis=-1).astype(jnp.bfloat16)
    scale = 1.0 / math.sqrt(total_sub * (W // 2))
    table = lag_rows(n_freq, scale).reshape(n_freq, 2, half_band, LAGS)
    table = jnp.asarray(table.transpose(1, 0, 2, 3).reshape(W, LAGS))
    corr = jnp.einsum("ijf,fl->ijl", spectra_cross, table, preferred_element_type=jnp.float32)
    corr = lax.all_to_all(
        corr.astype(jnp.bfloat16), "freq", split_axis=2, concat_axis=0, tiled=True
    )
    lags = LAGS // n_freq
    placed = jnp.dot(
        slot_onehot, corr.reshape(good_count, sources * lags), preferred_element_type=jnp.float32
    ).astype(jnp.bfloat16)
    placed = placed.reshape(n_chan, capacity, sources, lags)
    received = lax.all_to_all(placed, "chan", split_axis=0, concat_axis=0, tiled=True)
    return received.reshape(slot_count, sources, lags).astype(jnp.float32)


MESH = pl.DeviceIdType.MESH
CHUNKS = 2
LANES = 128


def column_order(bands):
    return np.arange(W).reshape(bands, 2, W // bands // 2).transpose(1, 0, 2).reshape(W)


def kernel(
    n_chan,
    n_freq,
    order_ref,
    picks_ref,
    dest_ref,
    good_ref,
    raw_ref,
    trans_hbm,
    table_hbm,
    out_ref,
    trans_ref,
    table_ref,
    share_out,
    share_in,
    panel_out,
    panel_in,
    panel_raw,
    spec_ref,
    white_ref,
    panel_ref,
    cross_ref,
    lag_out,
    lag_in,
    placed_ref,
    local_sems,
    share_send,
    share_recv,
    panel_send,
    panel_recv,
    gather_send,
    gather_recv,
    lag_send,
    lag_recv,
    place_send,
    place_recv,
):
    f32, bf16 = jnp.float32, jnp.bfloat16
    chan, freq = lax.axis_index("chan"), lax.axis_index("freq")
    raw_rows = raw_ref.shape[0]
    good_count = dest_ref.shape[1]
    share = good_count // n_freq
    capacity = 2 * good_count // n_chan
    slot_count = n_chan * capacity
    sub_count = raw_ref.shape[1] // W
    total_sub = sub_count * n_freq
    steps, per_step = picks_ref.shape
    sources = steps * per_step
    group = sources // CHUNKS
    half = W // 2
    lags = LAGS // n_freq

    load_trans = pltpu.make_async_copy(trans_hbm, trans_ref, local_sems.at[0])
    load_table = pltpu.make_async_copy(table_hbm, table_ref, local_sems.at[1])
    load_trans.start()
    load_table.start()

    def chan_peer(d):
        return lax.rem(chan + d, n_chan)

    def freq_peer(d):
        return lax.rem(freq + d, n_freq)

    barrier = pltpu.get_barrier_semaphore()
    for d in range(1, n_chan):
        pl.semaphore_signal(barrier, inc=1, device_id={"chan": chan_peer(d)}, device_id_type=MESH)
    for d in range(1, n_freq):
        pl.semaphore_signal(barrier, inc=1, device_id={"freq": freq_peer(d)}, device_id_type=MESH)

    good_col = jnp.transpose(
        jnp.broadcast_to(good_ref[...].astype(f32), (good_count, good_count))
    )[:, :1]
    row_onehot = (
        good_col == lax.broadcasted_iota(jnp.int32, (good_count, raw_rows), 1).astype(f32)
    ).astype(bf16)
    good = jnp.dot(row_onehot, raw_ref[...], preferred_element_type=f32).astype(bf16)
    for f in range(n_freq):
        share_out[f] = good[f * share : (f + 1) * share]
    dest_row = jnp.broadcast_to(dest_ref[...].astype(f32), (good_count, good_count))
    earlier = jnp.logical_and(
        dest_row == jnp.transpose(dest_row),
        lax.broadcasted_iota(jnp.int32, (good_count, good_count), 0)
        < lax.broadcasted_iota(jnp.int32, (good_count, good_count), 1),
    )
    earlier_count = jnp.sum(jnp.where(earlier, 1.0, 0.0), axis=0, keepdims=True)
    slot_index = dest_ref[...].astype(f32) * capacity + earlier_count

    source_row = lax.broadcasted_iota(jnp.int32, (sources, good_count), 0)
    source_slot = jnp.full((sources, good_count), -1, jnp.int32)
    for t in range(steps):
        for j in range(per_step):
            pick = picks_ref[t, j]
            slot = jnp.where(
                lax.div(pick, capacity) == chan, order_ref[t] * capacity + lax.rem(pick, capacity), -1
            )
            source_slot = jnp.where(source_row == t * per_step + j, slot, source_slot)
    source_onehot = (source_slot.astype(f32) == slot_index).astype(bf16)
    chosen = jnp.dot(source_onehot, good, preferred_element_type=f32)
    panel_out[...] = jnp.concatenate(
        [chosen[:, m * W : (m + 1) * W] for m in range(sub_count)], axis=0
    ).astype(bf16)

    pl.semaphore_wait(barrier, n_chan + n_freq - 2)

    pending = []

    def send(src, dst, send_sem, recv_sem, peer):
        copy = pltpu.make_async_remote_copy(
            src_ref=src,
            dst_ref=dst,
            send_sem=send_sem,
            recv_sem=recv_sem,
            device_id=peer,
            device_id_type=MESH,
        )
        copy.start()
        pending.append(copy)
        return copy

    panel_copies = [
        send(panel_out, panel_in.at[d - 1], panel_send.at[d - 1], panel_recv.at[d - 1],
             {"chan": chan_peer(d)})
        for d in range(1, n_chan)
    ]
    share_copies = [
        send(share_out.at[freq_peer(d)], share_in.at[d - 1], share_send.at[d - 1],
             share_recv.at[d - 1], {"freq": freq_peer(d)})
        for d in range(1, n_freq)
    ]
    load_trans.wait()

    def transform(rows, source):
        stacked = jnp.concatenate([rows[:, m * W : (m + 1) * W] for m in range(sub_count)], axis=0)
        spectra = jnp.dot(stacked, trans_ref[...], preferred_element_type=f32).astype(bf16)
        for m in range(sub_count):
            spec_ref[source * sub_count + m] = spectra[m * share : (m + 1) * share]

    for copy in panel_copies:
        copy.wait_recv()
    total = panel_out[...].astype(f32)
    for d in range(1, n_chan):
        total = total + panel_in[d - 1].astype(f32)
    panel_raw[freq] = total.astype(bf16)
    gather_copies = [
        send(panel_raw.at[freq], panel_raw.at[freq], gather_send.at[d - 1], gather_recv.at[d - 1],
             {"freq": freq_peer(d)})
        for d in range(1, n_freq)
    ]
    transform(share_out[freq], freq)
    for d in range(1, n_freq):
        share_copies[d - 1].wait_recv()
        transform(share_in[d - 1], freq_peer(n_freq - d))
    for copy in gather_copies:
        copy.wait_recv()

    def whiten_into(values, target):
        re, im = values[..., :half], values[..., half:]
        power = jnp.sum(re * re + im * im, axis=0, keepdims=True) * (1.0 / total_sub)
        factor = 1.0 / jnp.sqrt(jnp.maximum(power, power_floor))
        target[:, :, :half] = (re * factor).astype(bf16).astype(f32)
        target[:, :, half:] = (im * factor).astype(bf16).astype(f32)

    panel_spec = jnp.dot(
        panel_raw[...].reshape(total_sub * sources, W), trans_ref[...], preferred_element_type=f32
    ).astype(bf16).astype(f32)
    whiten_into(panel_spec.reshape(total_sub, sources, W), panel_ref)
    whiten_into(spec_ref[...].astype(f32), white_ref)
    load_table.wait()

    lag_copies = []
    for h in range(CHUNKS):

        def cross_bins(c, carry):
            at_re = pl.ds(pl.multiple_of(c * LANES, LANES), LANES)
            at_im = pl.ds(pl.multiple_of(half + c * LANES, LANES), LANES)
            left_re, left_im = white_ref[:, :, at_re], white_ref[:, :, at_im]
            for j in range(group):
                source = h * group + j
                right_re = panel_ref[:, source : source + 1, at_re]
                right_im = panel_ref[:, source : source + 1, at_im]
                real = jnp.sum(left_re * right_re + left_im * right_im, axis=0)
                imag = jnp.sum(left_im * right_re - left_re * right_im, axis=0)
                cross_ref[h, j * share : (j + 1) * share, at_re] = real.astype(bf16)
                cross_ref[h, j * share : (j + 1) * share, at_im] = imag.astype(bf16)
            return carry

        lax.fori_loop(0, half // LANES, cross_bins, 0)
        corr = jnp.dot(cross_ref[h], table_ref[...], preferred_element_type=f32).astype(bf16)
        for f in range(n_freq):
            lag_out[h, f] = corr[:, f * lags : (f + 1) * lags]
        lag_copies.append([
            send(lag_out.at[h, freq_peer(d)], lag_in.at[h, freq], lag_send.at[h, d - 1],
                 lag_recv.at[h, d - 1], {"freq": freq_peer(d)})
            for d in range(1, n_freq)
        ])
        lag_in[h, freq] = lag_out[h, freq]

    slot_onehot = (
        lax.broadcasted_iota(jnp.int32, (slot_count, good_count), 0).astype(f32) == slot_index
    ).astype(bf16)
    place_copies = []
    own_copies = []
    for h in range(CHUNKS):
        for copy in lag_copies[h]:
            copy.wait_recv()
        corr = jnp.concatenate(
            [
                jnp.concatenate(
                    [lag_in[h, f, j * share : (j + 1) * share] for f in range(n_freq)], axis=0
                )
                for j in range(group)
            ],
            axis=1,
        )
        placed = jnp.dot(slot_onehot, corr, preferred_element_type=f32).astype(bf16)
        for b in range(n_chan):
            placed_ref[h, b] = placed[b * capacity : (b + 1) * capacity]
        at = pl.ds(h * group * lags, group * lags)
        place_copies += [
            send(placed_ref.at[h, chan_peer(d)], out_ref.at[chan, :, at], place_send.at[h, d - 1],
                 place_recv.at[h, d - 1], {"chan": chan_peer(d)})
            for d in range(1, n_chan)
        ]
        own = pltpu.make_async_copy(
            placed_ref.at[h, chan], out_ref.at[chan, :, at], local_sems.at[2 + h]
        )
        own.start()
        own_copies.append(own)
    for copy in place_copies:
        copy.wait_recv()
    for own in own_copies:
        own.wait()
    for copy in pending:
        copy.wait_send()


def fused(raw, good_list, dest, order, picks):
    n_chan = lax.axis_size("chan")
    n_freq = lax.axis_size("freq")
    good_count = good_list.shape[0]
    share = good_count // n_freq
    capacity = 2 * good_count // n_chan
    sub_count = raw.shape[1] // W
    total_sub = sub_count * n_freq
    sources = picks.size
    group = sources // CHUNKS
    lags = LAGS // n_freq
    columns = column_order(n_freq)
    scale = 1.0 / math.sqrt(total_sub * (W // 2))
    trans = jnp.asarray(transform_table(n_freq)[:, columns])
    table = jnp.asarray(lag_rows(n_freq, scale)[columns])
    bf16, f32 = jnp.bfloat16, jnp.float32
    dma = pltpu.SemaphoreType.DMA
    vmem = pl.BlockSpec(memory_space=pltpu.VMEM)
    smem = pl.BlockSpec(memory_space=pltpu.SMEM)
    hbm = pl.BlockSpec(memory_space=pl.ANY)
    received = pl.pallas_call(
        functools.partial(kernel, n_chan, n_freq),
        out_shape=jax.ShapeDtypeStruct((n_chan, capacity, sources * lags), bf16),
        in_specs=[smem, smem, vmem, vmem, vmem, hbm, hbm],
        out_specs=hbm,
        scratch_shapes=[
            pltpu.VMEM((W, W), bf16),
            pltpu.VMEM((W, LAGS), bf16),
            pltpu.VMEM((n_freq, share, sub_count * W), bf16),
            pltpu.VMEM((n_freq - 1, share, sub_count * W), bf16),
            pltpu.VMEM((sub_count * sources, W), bf16),
            pltpu.VMEM((n_chan - 1, sub_count * sources, W), bf16),
            pltpu.VMEM((n_freq, sub_count * sources, W), bf16),
            pltpu.VMEM((total_sub, share, W), bf16),
            pltpu.VMEM((total_sub, share, W), f32),
            pltpu.VMEM((total_sub, sources, W), f32),
            pltpu.VMEM((CHUNKS, group * share, W), bf16),
            pltpu.VMEM((CHUNKS, n_freq, group * share, lags), bf16),
            pltpu.VMEM((CHUNKS, n_freq, group * share, lags), bf16),
            pltpu.VMEM((CHUNKS, n_chan, capacity, group * lags), bf16),
            dma((2 + CHUNKS,)),
            dma((n_freq - 1,)),
            dma((n_freq - 1,)),
            dma((n_chan - 1,)),
            dma((n_chan - 1,)),
            dma((n_freq - 1,)),
            dma((n_freq - 1,)),
            dma((CHUNKS, n_freq - 1)),
            dma((CHUNKS, n_freq - 1)),
            dma((CHUNKS, n_chan - 1)),
            dma((CHUNKS, n_chan - 1)),
        ],
        compiler_params=pltpu.CompilerParams(
            collective_id=0, has_side_effects=True, vmem_limit_bytes=40 * 1024 * 1024
        ),
    )(order, picks, dest.reshape(1, good_count), good_list.reshape(1, good_count), raw, trans, table)
    return received.reshape(n_chan * capacity, sources, lags).astype(f32)


def body(raw, good_list, dest, order, picks):
    n_chan = lax.axis_size("chan")
    n_freq = lax.axis_size("freq")
    capacity = 2 * good_list.shape[0] // n_chan
    if capacity % 16 == 0 and n_chan <= 16 and good_list.shape[0] == LANES:
        return fused(raw, good_list, dest, order, picks)
    return separate(raw, good_list, dest, order, picks)


def solution(mesh):
    placed = (P("chan", "freq"), P("chan"), P("chan"), P(), P())
    return jax.shard_map(
        body, mesh=mesh, in_specs=placed, out_specs=P("chan", None, "freq"), check_vma=False
    )
```

```python
import functools
import math

import jax
import jax.numpy as jnp
import ml_dtypes
import numpy as np
from jax import lax
from jax.experimental import pallas as pl
from jax.experimental.pallas import tpu as pltpu
from jax.sharding import PartitionSpec as P

W = 1024
LAGS = 512


power_floor = 0.1


def transform_table(bands):
    sample = np.arange(W, dtype=np.int64)[:, None]
    column = np.arange(W, dtype=np.int64)[None, :]
    width_band = W // bands
    half_band = width_band // 2
    within = column % width_band
    bin_index = (column // width_band) * half_band + within % half_band
    phase_rad = ((sample * bin_index) % W) * (2.0 * math.pi / W)
    taper = 0.5 - 0.5 * np.cos(sample * (2.0 * math.pi / W))
    entries = np.where(within < half_band, np.cos(phase_rad), -np.sin(phase_rad))
    return (entries * taper / math.sqrt(W)).astype(np.float32).astype(ml_dtypes.bfloat16)


def lag_rows(bands, scale):
    row_index = np.arange(W, dtype=np.int64)
    width_band = W // bands
    half_band = width_band // 2
    within = row_index % width_band
    bin_index = (row_index // width_band) * half_band + within % half_band
    lag_shift = np.arange(LAGS, dtype=np.int64) - LAGS // 2
    phase_rad = ((bin_index[:, None] * lag_shift[None, :]) % W) * (2.0 * math.pi / W)
    entries = np.where(within[:, None] < half_band, np.cos(phase_rad), -np.sin(phase_rad))
    return (entries * scale).astype(np.float32).astype(ml_dtypes.bfloat16)


def whiten(spectra):
    values = spectra.astype(jnp.float32)
    band_power = jnp.mean(jnp.sum(values * values, axis=-2, keepdims=True), axis=-3, keepdims=True)
    factor = 1.0 / jnp.sqrt(jnp.maximum(band_power, power_floor))
    return (values * factor).astype(jnp.bfloat16)


def separate(raw, good_list, dest, order, picks):
    n_chan = lax.axis_size("chan")
    n_freq = lax.axis_size("freq")
    good_count = good_list.shape[0]
    raw_rows = raw.shape[0]
    capacity = 2 * good_count // n_chan
    slot_count = n_chan * capacity
    sub_count = raw.shape[1] // W
    total_sub = sub_count * n_freq
    steps, per_step = picks.shape
    sources = steps * per_step
    share = good_count // n_freq
    positions = jnp.arange(good_count, dtype=jnp.int32)
    matching = dest[:, None] == dest[None, :]
    earlier_count = jnp.sum(
        jnp.logical_and(matching, positions[None, :] < positions[:, None]), axis=1
    )
    slot_index = dest * capacity + earlier_count
    row_onehot = (good_list[:, None] == jnp.arange(raw_rows, dtype=jnp.int32)[None, :]).astype(
        jnp.bfloat16
    )
    slot_onehot = (jnp.arange(slot_count, dtype=jnp.int32)[:, None] == slot_index[None, :]).astype(
        jnp.bfloat16
    )
    block = jnp.repeat(order, per_step)
    pick = picks.reshape(sources)
    mine = pick // capacity == lax.axis_index("chan")
    source_slot = jnp.where(mine, block * capacity + pick % capacity, -1)
    source_onehot = (source_slot[:, None] == slot_index[None, :]).astype(jnp.bfloat16)

    good = jnp.dot(row_onehot, raw, preferred_element_type=jnp.float32).astype(jnp.bfloat16)
    panel_raw = jnp.dot(source_onehot, good, preferred_element_type=jnp.float32).astype(jnp.bfloat16)
    panel_raw = lax.psum(panel_raw, "chan")
    panel_raw = lax.all_gather(panel_raw.reshape(sources, sub_count, W), "freq", axis=1, tiled=True)

    rows = lax.all_to_all(
        good.reshape(n_freq, share, sub_count, W), "freq", split_axis=0, concat_axis=2, tiled=True
    )
    rows = rows.reshape(share, total_sub, W)
    trans = jnp.asarray(transform_table(n_freq))
    half_band = W // n_freq // 2

    def white(values):
        spectra = jnp.einsum("cmw,wk->cmk", values, trans, preferred_element_type=jnp.float32)
        spectra = spectra.astype(jnp.bfloat16).reshape(-1, total_sub, n_freq, 2, half_band)
        spectra = spectra.transpose(0, 1, 3, 2, 4).reshape(-1, total_sub, 2, W // 2)
        return whiten(spectra).astype(jnp.float32)

    panels = white(panel_raw)
    whitened = white(rows)
    left_re, left_im = whitened[:, None, :, 0], whitened[:, None, :, 1]
    right_re, right_im = panels[None, :, :, 0], panels[None, :, :, 1]
    real_part = jnp.sum(left_re * right_re + left_im * right_im, axis=2)
    imag_part = jnp.sum(left_im * right_re - left_re * right_im, axis=2)
    spectra_cross = jnp.concatenate([real_part, imag_part], axis=-1).astype(jnp.bfloat16)
    scale = 1.0 / math.sqrt(total_sub * (W // 2))
    table = lag_rows(n_freq, scale).reshape(n_freq, 2, half_band, LAGS)
    table = jnp.asarray(table.transpose(1, 0, 2, 3).reshape(W, LAGS))
    corr = jnp.einsum("ijf,fl->ijl", spectra_cross, table, preferred_element_type=jnp.float32)
    corr = lax.all_to_all(
        corr.astype(jnp.bfloat16), "freq", split_axis=2, concat_axis=0, tiled=True
    )
    lags = LAGS // n_freq
    placed = jnp.dot(
        slot_onehot, corr.reshape(good_count, sources * lags), preferred_element_type=jnp.float32
    ).astype(jnp.bfloat16)
    placed = placed.reshape(n_chan, capacity, sources, lags)
    received = lax.all_to_all(placed, "chan", split_axis=0, concat_axis=0, tiled=True)
    return received.reshape(slot_count, sources, lags).astype(jnp.float32)


MESH = pl.DeviceIdType.MESH
CHUNKS = 2
LANES = 128


def column_order(bands):
    return np.arange(W).reshape(bands, 2, W // bands // 2).transpose(1, 0, 2).reshape(W)


def kernel(
    n_chan,
    n_freq,
    order_hbm,
    picks_hbm,
    dest_hbm,
    good_hbm,
    raw_hbm,
    trans_hbm,
    table_hbm,
    out_ref,
    order_ref,
    picks_ref,
    dest_ref,
    good_ref,
    raw_ref,
    trans_ref,
    table_ref,
    share_out,
    share_in,
    panel_out,
    panel_in,
    panel_raw,
    spec_ref,
    white_ref,
    panel_ref,
    cross_ref,
    lag_out,
    lag_in,
    placed_ref,
    local_sems,
    share_send,
    share_recv,
    panel_send,
    panel_recv,
    gather_send,
    gather_recv,
    lag_send,
    lag_recv,
    place_send,
    place_recv,
):
    f32, bf16 = jnp.float32, jnp.bfloat16
    chan, freq = lax.axis_index("chan"), lax.axis_index("freq")
    raw_rows = raw_ref.shape[0]
    good_count = dest_ref.shape[1]
    share = good_count // n_freq
    capacity = 2 * good_count // n_chan
    slot_count = n_chan * capacity
    sub_count = raw_ref.shape[1] // W
    total_sub = sub_count * n_freq
    per_step, steps = picks_ref.shape
    sources = steps * per_step
    group = sources // CHUNKS
    half = W // 2
    lags = LAGS // n_freq

    loads = [
        pltpu.make_async_copy(source, target, local_sems.at[2 + CHUNKS + i])
        for i, (source, target) in enumerate((
            (raw_hbm, raw_ref),
            (good_hbm, good_ref),
            (dest_hbm, dest_ref),
            (order_hbm, order_ref),
            (picks_hbm, picks_ref),
        ))
    ]
    for load in loads:
        load.start()
    load_trans = pltpu.make_async_copy(trans_hbm, trans_ref, local_sems.at[0])
    load_table = pltpu.make_async_copy(table_hbm, table_ref, local_sems.at[1])
    load_trans.start()
    load_table.start()

    def chan_peer(d):
        return lax.rem(chan + d, n_chan)

    def freq_peer(d):
        return lax.rem(freq + d, n_freq)

    barrier = pltpu.get_barrier_semaphore()
    for d in range(1, n_chan):
        pl.semaphore_signal(barrier, inc=1, device_id={"chan": chan_peer(d)}, device_id_type=MESH)
    for d in range(1, n_freq):
        pl.semaphore_signal(barrier, inc=1, device_id={"freq": freq_peer(d)}, device_id_type=MESH)

    for load in loads:
        load.wait()

    good_col = jnp.transpose(
        jnp.broadcast_to(good_ref[...].astype(f32), (good_count, good_count))
    )[:, :1]
    row_onehot = (
        good_col == lax.broadcasted_iota(jnp.int32, (good_count, raw_rows), 1).astype(f32)
    ).astype(bf16)
    good = jnp.dot(row_onehot, raw_ref[...], preferred_element_type=f32).astype(bf16)
    for f in range(n_freq):
        share_out[f] = good[f * share : (f + 1) * share]
    dest_row = jnp.broadcast_to(dest_ref[...].astype(f32), (good_count, good_count))
    earlier = jnp.logical_and(
        dest_row == jnp.transpose(dest_row),
        lax.broadcasted_iota(jnp.int32, (good_count, good_count), 0)
        < lax.broadcasted_iota(jnp.int32, (good_count, good_count), 1),
    )
    earlier_count = jnp.sum(jnp.where(earlier, 1.0, 0.0), axis=0, keepdims=True)
    slot_index = dest_ref[...].astype(f32) * capacity + earlier_count

    source_row = lax.broadcasted_iota(jnp.int32, (sources, good_count), 0)
    source_slot = jnp.full((sources, good_count), -1, jnp.int32)
    for t in range(steps):
        for j in range(per_step):
            pick = picks_ref[j, t]
            slot = jnp.where(
                lax.div(pick, capacity) == chan, order_ref[t] * capacity + lax.rem(pick, capacity), -1
            )
            source_slot = jnp.where(source_row == t * per_step + j, slot, source_slot)
    source_onehot = (source_slot.astype(f32) == slot_index).astype(bf16)
    chosen = jnp.dot(source_onehot, good, preferred_element_type=f32)
    panel_out[...] = jnp.concatenate(
        [chosen[:, m * W : (m + 1) * W] for m in range(sub_count)], axis=0
    ).astype(bf16)

    pl.semaphore_wait(barrier, n_chan + n_freq - 2)

    pending = []

    def send(src, dst, send_sem, recv_sem, peer):
        copy = pltpu.make_async_remote_copy(
            src_ref=src,
            dst_ref=dst,
            send_sem=send_sem,
            recv_sem=recv_sem,
            device_id=peer,
            device_id_type=MESH,
        )
        copy.start()
        pending.append(copy)
        return copy

    panel_copies = [
        send(panel_out, panel_in.at[d - 1], panel_send.at[d - 1], panel_recv.at[d - 1],
             {"chan": chan_peer(d)})
        for d in range(1, n_chan)
    ]
    share_copies = [
        send(share_out.at[freq_peer(d)], share_in.at[d - 1], share_send.at[d - 1],
             share_recv.at[d - 1], {"freq": freq_peer(d)})
        for d in range(1, n_freq)
    ]
    load_trans.wait()

    def transform(rows, source):
        stacked = jnp.concatenate([rows[:, m * W : (m + 1) * W] for m in range(sub_count)], axis=0)
        spectra = jnp.dot(stacked, trans_ref[...], preferred_element_type=f32).astype(bf16)
        for m in range(sub_count):
            spec_ref[source * sub_count + m] = spectra[m * share : (m + 1) * share]

    for copy in panel_copies:
        copy.wait_recv()
    total = panel_out[...].astype(f32)
    for d in range(1, n_chan):
        total = total + panel_in[d - 1].astype(f32)
    panel_raw[freq] = total.astype(bf16)
    gather_copies = [
        send(panel_raw.at[freq], panel_raw.at[freq], gather_send.at[d - 1], gather_recv.at[d - 1],
             {"freq": freq_peer(d)})
        for d in range(1, n_freq)
    ]
    transform(share_out[freq], freq)
    for d in range(1, n_freq):
        share_copies[d - 1].wait_recv()
        transform(share_in[d - 1], freq_peer(n_freq - d))
    for copy in gather_copies:
        copy.wait_recv()

    def whiten_into(values, target):
        re, im = values[..., :half], values[..., half:]
        power = jnp.sum(re * re + im * im, axis=0, keepdims=True) * (1.0 / total_sub)
        factor = 1.0 / jnp.sqrt(jnp.maximum(power, power_floor))
        target[:, :, :half] = (re * factor).astype(bf16).astype(f32)
        target[:, :, half:] = (im * factor).astype(bf16).astype(f32)

    panel_spec = jnp.dot(
        panel_raw[...].reshape(total_sub * sources, W), trans_ref[...], preferred_element_type=f32
    ).astype(bf16).astype(f32)
    whiten_into(panel_spec.reshape(total_sub, sources, W), panel_ref)
    whiten_into(spec_ref[...].astype(f32), white_ref)
    load_table.wait()

    lag_copies = []
    for h in range(CHUNKS):

        def cross_bins(c, carry):
            at_re = pl.ds(pl.multiple_of(c * LANES, LANES), LANES)
            at_im = pl.ds(pl.multiple_of(half + c * LANES, LANES), LANES)
            left_re, left_im = white_ref[:, :, at_re], white_ref[:, :, at_im]
            for j in range(group):
                source = h * group + j
                right_re = panel_ref[:, source : source + 1, at_re]
                right_im = panel_ref[:, source : source + 1, at_im]
                real = jnp.sum(left_re * right_re + left_im * right_im, axis=0)
                imag = jnp.sum(left_im * right_re - left_re * right_im, axis=0)
                cross_ref[h, j * share : (j + 1) * share, at_re] = real.astype(bf16)
                cross_ref[h, j * share : (j + 1) * share, at_im] = imag.astype(bf16)
            return carry

        lax.fori_loop(0, half // LANES, cross_bins, 0)
        corr = jnp.dot(cross_ref[h], table_ref[...], preferred_element_type=f32).astype(bf16)
        for f in range(n_freq):
            lag_out[h, f] = corr[:, f * lags : (f + 1) * lags]
        lag_copies.append([
            send(lag_out.at[h, freq_peer(d)], lag_in.at[h, freq], lag_send.at[h, d - 1],
                 lag_recv.at[h, d - 1], {"freq": freq_peer(d)})
            for d in range(1, n_freq)
        ])
        lag_in[h, freq] = lag_out[h, freq]

    slot_onehot = (
        lax.broadcasted_iota(jnp.int32, (slot_count, good_count), 0).astype(f32) == slot_index
    ).astype(bf16)
    place_copies = []
    own_copies = []
    for h in range(CHUNKS):
        for copy in lag_copies[h]:
            copy.wait_recv()
        corr = jnp.concatenate(
            [
                jnp.concatenate(
                    [lag_in[h, f, j * share : (j + 1) * share] for f in range(n_freq)], axis=0
                )
                for j in range(group)
            ],
            axis=1,
        )
        placed = jnp.dot(slot_onehot, corr, preferred_element_type=f32).astype(bf16)
        for b in range(n_chan):
            placed_ref[h, b] = placed[b * capacity : (b + 1) * capacity]
        at = pl.ds(h * group * lags, group * lags)
        place_copies += [
            send(placed_ref.at[h, chan_peer(d)], out_ref.at[chan, :, at], place_send.at[h, d - 1],
                 place_recv.at[h, d - 1], {"chan": chan_peer(d)})
            for d in range(1, n_chan)
        ]
        own = pltpu.make_async_copy(
            placed_ref.at[h, chan], out_ref.at[chan, :, at], local_sems.at[2 + h]
        )
        own.start()
        own_copies.append(own)
    for copy in place_copies:
        copy.wait_recv()
    for own in own_copies:
        own.wait()
    for copy in pending:
        copy.wait_send()


def fused(raw, good_list, dest, order, picks):
    n_chan = lax.axis_size("chan")
    n_freq = lax.axis_size("freq")
    good_count = good_list.shape[0]
    share = good_count // n_freq
    capacity = 2 * good_count // n_chan
    sub_count = raw.shape[1] // W
    total_sub = sub_count * n_freq
    sources = picks.size
    group = sources // CHUNKS
    lags = LAGS // n_freq
    columns = column_order(n_freq)
    scale = 1.0 / math.sqrt(total_sub * (W // 2))
    trans = jnp.asarray(transform_table(n_freq)[:, columns])
    table = jnp.asarray(lag_rows(n_freq, scale)[columns])
    bf16, f32 = jnp.bfloat16, jnp.float32
    dma = pltpu.SemaphoreType.DMA
    hbm = pl.BlockSpec(memory_space=pltpu.HBM)
    received = pl.pallas_call(
        functools.partial(kernel, n_chan, n_freq),
        out_shape=jax.ShapeDtypeStruct((n_chan, capacity, sources * lags), bf16),
        in_specs=[hbm] * 7,
        out_specs=pl.BlockSpec(memory_space=pl.ANY),
        scratch_shapes=[
            pltpu.SMEM(order.shape, jnp.int32),
            pltpu.SMEM(picks.shape[::-1], jnp.int32),
            pltpu.VMEM((1, good_count), jnp.int32),
            pltpu.VMEM((1, good_count), jnp.int32),
            pltpu.VMEM(raw.shape, bf16),
            pltpu.VMEM((W, W), bf16),
            pltpu.VMEM((W, LAGS), bf16),
            pltpu.VMEM((n_freq, share, sub_count * W), bf16),
            pltpu.VMEM((n_freq - 1, share, sub_count * W), bf16),
            pltpu.VMEM((sub_count * sources, W), bf16),
            pltpu.VMEM((n_chan - 1, sub_count * sources, W), bf16),
            pltpu.VMEM((n_freq, sub_count * sources, W), bf16),
            pltpu.VMEM((total_sub, share, W), bf16),
            pltpu.VMEM((total_sub, share, W), f32),
            pltpu.VMEM((total_sub, sources, W), f32),
            pltpu.VMEM((CHUNKS, group * share, W), bf16),
            pltpu.VMEM((CHUNKS, n_freq, group * share, lags), bf16),
            pltpu.VMEM((CHUNKS, n_freq, group * share, lags), bf16),
            pltpu.VMEM((CHUNKS, n_chan, capacity, group * lags), bf16),
            dma((7 + CHUNKS,)),
            dma((n_freq - 1,)),
            dma((n_freq - 1,)),
            dma((n_chan - 1,)),
            dma((n_chan - 1,)),
            dma((n_freq - 1,)),
            dma((n_freq - 1,)),
            dma((CHUNKS, n_freq - 1)),
            dma((CHUNKS, n_freq - 1)),
            dma((CHUNKS, n_chan - 1)),
            dma((CHUNKS, n_chan - 1)),
        ],
        compiler_params=pltpu.CompilerParams(
            collective_id=0, has_side_effects=True, vmem_limit_bytes=63 * 1024 * 1024
        ),
    )(order, picks.T, dest.reshape(1, good_count), good_list.reshape(1, good_count), raw, trans, table)
    return received.reshape(n_chan * capacity, sources, lags).astype(f32)


def body(raw, good_list, dest, order, picks):
    n_chan = lax.axis_size("chan")
    n_freq = lax.axis_size("freq")
    capacity = 2 * good_list.shape[0] // n_chan
    if capacity % 16 == 0 and n_chan <= 16 and good_list.shape[0] == LANES:
        return fused(raw, good_list, dest, order, picks)
    return separate(raw, good_list, dest, order, picks)


def solution(mesh):
    placed = (P("chan", "freq"), P("chan"), P("chan"), P(), P())
    return jax.shard_map(
        body, mesh=mesh, in_specs=placed, out_specs=P("chan", None, "freq"), check_vma=False
    )
```

```python
import functools
import math

import jax
import jax.numpy as jnp
import ml_dtypes
import numpy as np
from jax import lax
from jax.experimental import pallas as pl
from jax.experimental.pallas import tpu as pltpu
from jax.sharding import PartitionSpec as P

W = 1024
LAGS = 512


power_floor = 0.1


def transform_table(bands):
    sample = np.arange(W, dtype=np.int64)[:, None]
    column = np.arange(W, dtype=np.int64)[None, :]
    width_band = W // bands
    half_band = width_band // 2
    within = column % width_band
    bin_index = (column // width_band) * half_band + within % half_band
    phase_rad = ((sample * bin_index) % W) * (2.0 * math.pi / W)
    taper = 0.5 - 0.5 * np.cos(sample * (2.0 * math.pi / W))
    entries = np.where(within < half_band, np.cos(phase_rad), -np.sin(phase_rad))
    return (entries * taper / math.sqrt(W)).astype(np.float32).astype(ml_dtypes.bfloat16)


def lag_rows(bands, scale):
    row_index = np.arange(W, dtype=np.int64)
    width_band = W // bands
    half_band = width_band // 2
    within = row_index % width_band
    bin_index = (row_index // width_band) * half_band + within % half_band
    lag_shift = np.arange(LAGS, dtype=np.int64) - LAGS // 2
    phase_rad = ((bin_index[:, None] * lag_shift[None, :]) % W) * (2.0 * math.pi / W)
    entries = np.where(within[:, None] < half_band, np.cos(phase_rad), -np.sin(phase_rad))
    return (entries * scale).astype(np.float32).astype(ml_dtypes.bfloat16)


def whiten(spectra):
    values = spectra.astype(jnp.float32)
    band_power = jnp.mean(jnp.sum(values * values, axis=-2, keepdims=True), axis=-3, keepdims=True)
    factor = 1.0 / jnp.sqrt(jnp.maximum(band_power, power_floor))
    return (values * factor).astype(jnp.bfloat16)


def separate(raw, good_list, dest, order, picks):
    n_chan = lax.axis_size("chan")
    n_freq = lax.axis_size("freq")
    good_count = good_list.shape[0]
    raw_rows = raw.shape[0]
    capacity = 2 * good_count // n_chan
    slot_count = n_chan * capacity
    sub_count = raw.shape[1] // W
    total_sub = sub_count * n_freq
    steps, per_step = picks.shape
    sources = steps * per_step
    share = good_count // n_freq
    positions = jnp.arange(good_count, dtype=jnp.int32)
    matching = dest[:, None] == dest[None, :]
    earlier_count = jnp.sum(
        jnp.logical_and(matching, positions[None, :] < positions[:, None]), axis=1
    )
    slot_index = dest * capacity + earlier_count
    row_onehot = (good_list[:, None] == jnp.arange(raw_rows, dtype=jnp.int32)[None, :]).astype(
        jnp.bfloat16
    )
    slot_onehot = (jnp.arange(slot_count, dtype=jnp.int32)[:, None] == slot_index[None, :]).astype(
        jnp.bfloat16
    )
    block = jnp.repeat(order, per_step)
    pick = picks.reshape(sources)
    mine = pick // capacity == lax.axis_index("chan")
    source_slot = jnp.where(mine, block * capacity + pick % capacity, -1)
    source_onehot = (source_slot[:, None] == slot_index[None, :]).astype(jnp.bfloat16)

    good = jnp.dot(row_onehot, raw, preferred_element_type=jnp.float32).astype(jnp.bfloat16)
    panel_raw = jnp.dot(source_onehot, good, preferred_element_type=jnp.float32).astype(jnp.bfloat16)
    panel_raw = lax.psum(panel_raw, "chan")
    panel_raw = lax.all_gather(panel_raw.reshape(sources, sub_count, W), "freq", axis=1, tiled=True)

    rows = lax.all_to_all(
        good.reshape(n_freq, share, sub_count, W), "freq", split_axis=0, concat_axis=2, tiled=True
    )
    rows = rows.reshape(share, total_sub, W)
    trans = jnp.asarray(transform_table(n_freq))
    half_band = W // n_freq // 2

    def white(values):
        spectra = jnp.einsum("cmw,wk->cmk", values, trans, preferred_element_type=jnp.float32)
        spectra = spectra.astype(jnp.bfloat16).reshape(-1, total_sub, n_freq, 2, half_band)
        spectra = spectra.transpose(0, 1, 3, 2, 4).reshape(-1, total_sub, 2, W // 2)
        return whiten(spectra).astype(jnp.float32)

    panels = white(panel_raw)
    whitened = white(rows)
    left_re, left_im = whitened[:, None, :, 0], whitened[:, None, :, 1]
    right_re, right_im = panels[None, :, :, 0], panels[None, :, :, 1]
    real_part = jnp.sum(left_re * right_re + left_im * right_im, axis=2)
    imag_part = jnp.sum(left_im * right_re - left_re * right_im, axis=2)
    spectra_cross = jnp.concatenate([real_part, imag_part], axis=-1).astype(jnp.bfloat16)
    scale = 1.0 / math.sqrt(total_sub * (W // 2))
    table = lag_rows(n_freq, scale).reshape(n_freq, 2, half_band, LAGS)
    table = jnp.asarray(table.transpose(1, 0, 2, 3).reshape(W, LAGS))
    corr = jnp.einsum("ijf,fl->ijl", spectra_cross, table, preferred_element_type=jnp.float32)
    corr = lax.all_to_all(
        corr.astype(jnp.bfloat16), "freq", split_axis=2, concat_axis=0, tiled=True
    )
    lags = LAGS // n_freq
    placed = jnp.dot(
        slot_onehot, corr.reshape(good_count, sources * lags), preferred_element_type=jnp.float32
    ).astype(jnp.bfloat16)
    placed = placed.reshape(n_chan, capacity, sources, lags)
    received = lax.all_to_all(placed, "chan", split_axis=0, concat_axis=0, tiled=True)
    return received.reshape(slot_count, sources, lags).astype(jnp.float32)


MESH = pl.DeviceIdType.MESH
CHUNKS = 2
PORTIONS = 1
LANES = 128


def column_order(bands):
    return np.arange(W).reshape(bands, 2, W // bands // 2).transpose(1, 0, 2).reshape(W)


def kernel(
    n_chan,
    n_freq,
    order_hbm,
    picks_hbm,
    dest_hbm,
    good_hbm,
    raw_hbm,
    trans_hbm,
    table_hbm,
    out_ref,
    order_ref,
    picks_ref,
    dest_ref,
    good_ref,
    raw_ref,
    trans_ref,
    table_ref,
    share_out,
    share_in,
    panel_out,
    panel_in,
    panel_raw,
    white_ref,
    panel_ref,
    cross_ref,
    lag_out,
    lag_in,
    placed_ref,
    local_sems,
    share_send,
    share_recv,
    panel_send,
    panel_recv,
    gather_send,
    gather_recv,
    lag_send,
    lag_recv,
    place_send,
    place_recv,
):
    f32, bf16 = jnp.float32, jnp.bfloat16
    chan, freq = lax.axis_index("chan"), lax.axis_index("freq")
    raw_rows = raw_ref.shape[0]
    good_count = dest_ref.shape[1]
    share = good_count // n_freq
    portion = share // PORTIONS
    capacity = 2 * good_count // n_chan
    slot_count = n_chan * capacity
    sub_count = raw_ref.shape[1] // W
    total_sub = sub_count * n_freq
    per_step, steps = picks_ref.shape
    sources = steps * per_step
    group = sources // CHUNKS
    half = W // 2
    lags = LAGS // n_freq

    loads = [
        pltpu.make_async_copy(source, target, local_sems.at[2 + CHUNKS + i])
        for i, (source, target) in enumerate((
            (raw_hbm, raw_ref),
            (good_hbm, good_ref),
            (dest_hbm, dest_ref),
            (order_hbm, order_ref),
            (picks_hbm, picks_ref),
        ))
    ]
    for load in loads:
        load.start()
    load_trans = pltpu.make_async_copy(trans_hbm, trans_ref, local_sems.at[0])
    load_table = pltpu.make_async_copy(table_hbm, table_ref, local_sems.at[1])
    load_trans.start()
    load_table.start()

    def chan_peer(d):
        return lax.rem(chan + d, n_chan)

    def freq_peer(d):
        return lax.rem(freq + d, n_freq)

    barrier = pltpu.get_barrier_semaphore()
    for d in range(1, n_chan):
        pl.semaphore_signal(barrier, inc=1, device_id={"chan": chan_peer(d)}, device_id_type=MESH)
    for d in range(1, n_freq):
        pl.semaphore_signal(barrier, inc=1, device_id={"freq": freq_peer(d)}, device_id_type=MESH)

    for load in loads:
        load.wait()

    good_col = jnp.transpose(
        jnp.broadcast_to(good_ref[...].astype(f32), (good_count, good_count))
    )[:, :1]
    row_onehot = (
        good_col == lax.broadcasted_iota(jnp.int32, (good_count, raw_rows), 1).astype(f32)
    ).astype(bf16)
    good = jnp.dot(row_onehot, raw_ref[...], preferred_element_type=f32).astype(bf16)
    for g in range(PORTIONS):
        for f in range(n_freq):
            first = f * share + g * portion
            share_out[g, f] = good[first : first + portion]
    dest_row = jnp.broadcast_to(dest_ref[...].astype(f32), (good_count, good_count))
    earlier = jnp.logical_and(
        dest_row == jnp.transpose(dest_row),
        lax.broadcasted_iota(jnp.int32, (good_count, good_count), 0)
        < lax.broadcasted_iota(jnp.int32, (good_count, good_count), 1),
    )
    earlier_count = jnp.sum(jnp.where(earlier, 1.0, 0.0), axis=0, keepdims=True)
    slot_index = dest_ref[...].astype(f32) * capacity + earlier_count

    source_row = lax.broadcasted_iota(jnp.int32, (sources, good_count), 0)
    source_slot = jnp.full((sources, good_count), -1, jnp.int32)
    for t in range(steps):
        for j in range(per_step):
            pick = picks_ref[j, t]
            slot = jnp.where(
                lax.div(pick, capacity) == chan, order_ref[t] * capacity + lax.rem(pick, capacity), -1
            )
            source_slot = jnp.where(source_row == t * per_step + j, slot, source_slot)
    source_onehot = (source_slot.astype(f32) == slot_index).astype(bf16)
    chosen = jnp.dot(source_onehot, good, preferred_element_type=f32)
    panel_out[...] = jnp.concatenate(
        [chosen[:, m * W : (m + 1) * W] for m in range(sub_count)], axis=0
    ).astype(bf16)

    pl.semaphore_wait(barrier, n_chan + n_freq - 2)

    pending = []

    def send(src, dst, send_sem, recv_sem, peer):
        copy = pltpu.make_async_remote_copy(
            src_ref=src,
            dst_ref=dst,
            send_sem=send_sem,
            recv_sem=recv_sem,
            device_id=peer,
            device_id_type=MESH,
        )
        copy.start()
        pending.append(copy)
        return copy

    panel_copies = [
        send(panel_out, panel_in.at[d - 1], panel_send.at[d - 1], panel_recv.at[d - 1],
             {"chan": chan_peer(d)})
        for d in range(1, n_chan)
    ]
    def send_shares(g):
        return [
            send(share_out.at[g, freq_peer(d)], share_in.at[g, freq], share_send.at[g, d - 1],
                 share_recv.at[g, d - 1], {"freq": freq_peer(d)})
            for d in range(1, n_freq)
        ]

    share_copies = [send_shares(g) for g in range(PORTIONS)]
    for g in range(PORTIONS):
        share_in[g, freq] = share_out[g, freq]
    for copy in panel_copies:
        copy.wait_recv()
    total = panel_out[...].astype(f32)
    for d in range(1, n_chan):
        total = total + panel_in[d - 1].astype(f32)
    panel_raw[freq] = total.astype(bf16)
    gather_copies = [
        send(panel_raw.at[freq], panel_raw.at[freq], gather_send.at[d - 1], gather_recv.at[d - 1],
             {"freq": freq_peer(d)})
        for d in range(1, n_freq)
    ]
    load_trans.wait()

    def whiten_into(values, target):
        re, im = values[..., :half], values[..., half:]
        power = jnp.sum(re * re + im * im, axis=0, keepdims=True) * (1.0 / total_sub)
        factor = 1.0 / jnp.sqrt(jnp.maximum(power, power_floor))
        target[:, :, :half] = (re * factor).astype(bf16).astype(f32)
        target[:, :, half:] = (im * factor).astype(bf16).astype(f32)

    def transform(g):
        for copy in share_copies[g]:
            copy.wait_recv()
        stacked = jnp.concatenate(
            [
                share_in[g, f, :, m * W : (m + 1) * W]
                for f in range(n_freq)
                for m in range(sub_count)
            ],
            axis=0,
        )
        spectra = jnp.dot(stacked, trans_ref[...], preferred_element_type=f32).astype(bf16)
        whiten_into(spectra.astype(f32).reshape(total_sub, portion, W), white_ref.at[g])

    lag_copies = []

    def lag_part(g, first, count):
        def cross_bins(c, carry):
            at_re = pl.ds(pl.multiple_of(c * LANES, LANES), LANES)
            at_im = pl.ds(pl.multiple_of(half + c * LANES, LANES), LANES)
            left_re, left_im = white_ref[g, :, :, at_re], white_ref[g, :, :, at_im]
            for j in range(first, first + count):
                right_re = panel_ref[:, j : j + 1, at_re]
                right_im = panel_ref[:, j : j + 1, at_im]
                real = jnp.sum(left_re * right_re + left_im * right_im, axis=0)
                imag = jnp.sum(left_im * right_re - left_re * right_im, axis=0)
                cross_ref[g, j * portion : (j + 1) * portion, at_re] = real.astype(bf16)
                cross_ref[g, j * portion : (j + 1) * portion, at_im] = imag.astype(bf16)
            return carry

        lax.fori_loop(0, half // LANES, cross_bins, 0)
        rows = slice(first * portion, (first + count) * portion)
        at = pl.ds(first * portion, count * portion)
        part = len(lag_copies)
        corr = jnp.dot(cross_ref[g, rows], table_ref[...], preferred_element_type=f32).astype(bf16)
        for f in range(n_freq):
            lag_out[g, f, rows] = corr[:, f * lags : (f + 1) * lags]
        lag_copies.append([
            send(lag_out.at[g, freq_peer(d), at], lag_in.at[g, freq, at], lag_send.at[part, d - 1],
                 lag_recv.at[part, d - 1], {"freq": freq_peer(d)})
            for d in range(1, n_freq)
        ])
        lag_in[g, freq, rows] = lag_out[g, freq, rows]

    transform(0)
    for copy in gather_copies:
        copy.wait_recv()
    panel_spec = jnp.dot(
        panel_raw[...].reshape(total_sub * sources, W), trans_ref[...], preferred_element_type=f32
    ).astype(bf16).astype(f32)
    whiten_into(panel_spec.reshape(total_sub, sources, W), panel_ref)
    load_table.wait()
    for g in range(PORTIONS - 1):
        lag_part(g, 0, sources)
        transform(g + 1)
    for h in range(CHUNKS):
        lag_part(PORTIONS - 1, h * group, group)

    slot_onehot = (
        lax.broadcasted_iota(jnp.int32, (slot_count, good_count), 0).astype(f32) == slot_index
    ).astype(bf16)
    place_copies = []
    own_copies = []
    for h in range(CHUNKS):
        for part in range(PORTIONS - 1 + h if h else 0, PORTIONS + h):
            for copy in lag_copies[part]:
                copy.wait_recv()
        corr = jnp.concatenate(
            [
                jnp.concatenate(
                    [
                        lag_in[g, f, j * portion : (j + 1) * portion]
                        for f in range(n_freq)
                        for g in range(PORTIONS)
                    ],
                    axis=0,
                )
                for j in range(h * group, (h + 1) * group)
            ],
            axis=1,
        )
        placed = jnp.dot(slot_onehot, corr, preferred_element_type=f32).astype(bf16)
        for b in range(n_chan):
            placed_ref[h, b] = placed[b * capacity : (b + 1) * capacity]
        at = pl.ds(h * group * lags, group * lags)
        place_copies += [
            send(placed_ref.at[h, chan_peer(d)], out_ref.at[chan, :, at], place_send.at[h, d - 1],
                 place_recv.at[h, d - 1], {"chan": chan_peer(d)})
            for d in range(1, n_chan)
        ]
        own = pltpu.make_async_copy(
            placed_ref.at[h, chan], out_ref.at[chan, :, at], local_sems.at[2 + h]
        )
        own.start()
        own_copies.append(own)
    for copy in place_copies:
        copy.wait_recv()
    for own in own_copies:
        own.wait()
    for copy in pending:
        copy.wait_send()


def fused(raw, good_list, dest, order, picks):
    n_chan = lax.axis_size("chan")
    n_freq = lax.axis_size("freq")
    good_count = good_list.shape[0]
    share = good_count // n_freq
    capacity = 2 * good_count // n_chan
    sub_count = raw.shape[1] // W
    total_sub = sub_count * n_freq
    sources = picks.size
    group = sources // CHUNKS
    portion = share // PORTIONS
    lags = LAGS // n_freq
    columns = column_order(n_freq)
    scale = 1.0 / math.sqrt(total_sub * (W // 2))
    trans = jnp.asarray(transform_table(n_freq)[:, columns])
    table = jnp.asarray(lag_rows(n_freq, scale)[columns])
    bf16, f32 = jnp.bfloat16, jnp.float32
    dma = pltpu.SemaphoreType.DMA
    hbm = pl.BlockSpec(memory_space=pltpu.HBM)
    received = pl.pallas_call(
        functools.partial(kernel, n_chan, n_freq),
        out_shape=jax.ShapeDtypeStruct((n_chan, capacity, sources * lags), bf16),
        in_specs=[hbm] * 7,
        out_specs=pl.BlockSpec(memory_space=pl.ANY),
        scratch_shapes=[
            pltpu.SMEM(order.shape, jnp.int32),
            pltpu.SMEM(picks.shape[::-1], jnp.int32),
            pltpu.VMEM((1, good_count), jnp.int32),
            pltpu.VMEM((1, good_count), jnp.int32),
            pltpu.VMEM(raw.shape, bf16),
            pltpu.VMEM((W, W), bf16),
            pltpu.VMEM((W, LAGS), bf16),
            pltpu.VMEM((PORTIONS, n_freq, portion, sub_count * W), bf16),
            pltpu.VMEM((PORTIONS, n_freq, portion, sub_count * W), bf16),
            pltpu.VMEM((sub_count * sources, W), bf16),
            pltpu.VMEM((n_chan - 1, sub_count * sources, W), bf16),
            pltpu.VMEM((n_freq, sub_count * sources, W), bf16),
            pltpu.VMEM((PORTIONS, total_sub, portion, W), f32),
            pltpu.VMEM((total_sub, sources, W), f32),
            pltpu.VMEM((PORTIONS, sources * portion, W), bf16),
            pltpu.VMEM((PORTIONS, n_freq, sources * portion, lags), bf16),
            pltpu.VMEM((PORTIONS, n_freq, sources * portion, lags), bf16),
            pltpu.VMEM((CHUNKS, n_chan, capacity, group * lags), bf16),
            dma((7 + CHUNKS,)),
            dma((PORTIONS, n_freq - 1)),
            dma((PORTIONS, n_freq - 1)),
            dma((n_chan - 1,)),
            dma((n_chan - 1,)),
            dma((n_freq - 1,)),
            dma((n_freq - 1,)),
            dma((PORTIONS - 1 + CHUNKS, n_freq - 1)),
            dma((PORTIONS - 1 + CHUNKS, n_freq - 1)),
            dma((CHUNKS, n_chan - 1)),
            dma((CHUNKS, n_chan - 1)),
        ],
        compiler_params=pltpu.CompilerParams(
            collective_id=0, has_side_effects=True, vmem_limit_bytes=63 * 1024 * 1024
        ),
    )(order, picks.T, dest.reshape(1, good_count), good_list.reshape(1, good_count), raw, trans, table)
    return received.reshape(n_chan * capacity, sources, lags).astype(f32)


def body(raw, good_list, dest, order, picks):
    n_chan = lax.axis_size("chan")
    n_freq = lax.axis_size("freq")
    capacity = 2 * good_list.shape[0] // n_chan
    if capacity % 16 == 0 and n_chan <= 16 and good_list.shape[0] == LANES:
        return fused(raw, good_list, dest, order, picks)
    return separate(raw, good_list, dest, order, picks)


def solution(mesh):
    placed = (P("chan", "freq"), P("chan"), P("chan"), P(), P())
    return jax.shard_map(
        body, mesh=mesh, in_specs=placed, out_specs=P("chan", None, "freq"), check_vma=False
    )
```
